32 devices in a mesh: seg: 8 (over y, x, core), row: 4 (over z).
Axes of the slice: x: 2, y: 2, z: 4, core: 2. Of those that a mesh axis runs over, the one named last changes fastest.
Arguments:
- left_env: bfloat16 [8, 512, 12, 512], P('seg', 'row'), may hold values from -4 to 4, as said below
- right_env: bfloat16 [8, 512, 12, 512], P('seg'), may hold values from -4 to 4, as said below
- site_operator: bfloat16 [4, 12, 12, 4], replicated, may hold values from -1 to 2, as said below
- start_vector: float32 [8, 512, 4, 512], P('seg', 'row'), may hold values from -6 to 6
Outputs:
- last_vector: float32 [8, 512, 4, 512], P('seg', 'row')
- alpha_values: float32 [8, 2], P('seg')
- beta_values: float32 [8, 2], P('seg')
The draws below stay inside these ranges and needn't reach their ends.
Inputs may be any that keep to these rules, and one draw needn't show every extreme that they name: left_env[i, a, w, c] = left_env[i, c, w, a]. right_env[i, a, w, c] = right_env[i, c, w, a]. site_operator[s, v, w, r] = site_operator[r, v, w, s].
All inputs are finite; a program needn't handle non-finite values.
Results may differ from the reference program's by a relative error of at most 0.0076.
Values may be sent and summed in bfloat16 or wider, within the bound.
A program may use at most 128 MiB of HBM per device.

```python
import math
import jax
import jax.numpy as jnp
from jax import lax

D = 512
W = 12
DP = 4
ITERS = 2
SEGS = 8


def environment_draw(key, factor):
    key_noise = jax.random.fold_in(key, 0)
    normal_part = jnp.clip(jax.random.normal(key_noise, (SEGS, D, W, D), jnp.float32), -3.0, 3.0)
    symmetric = (normal_part + jnp.transpose(normal_part, (0, 3, 2, 1))) * (0.7 * factor / math.sqrt(D))
    rows_index = lax.broadcasted_iota(jnp.int32, (SEGS, D, W, D), 1)
    cols_index = lax.broadcasted_iota(jnp.int32, (SEGS, D, W, D), 3)
    chan_index = lax.broadcasted_iota(jnp.int32, (SEGS, D, W, D), 2)
    identity_part = jnp.where((rows_index == cols_index) & (chan_index == 0), 1.0, 0.0).astype(jnp.float32)
    return (symmetric + identity_part).astype(jnp.bfloat16)


def draw_left_env(key, part):
    return environment_draw(jax.random.fold_in(key, 11), 1.0)


def draw_right_env(key, part):
    return environment_draw(jax.random.fold_in(key, 23), 1.0 / math.sqrt(W))


def draw_site_operator(key, part):
    inner_key = jax.random.fold_in(key, 37)
    raw_part = jnp.clip(jax.random.normal(inner_key, (DP, W, W, DP), jnp.float32), -3.0, 3.0)
    symmetric = (raw_part + jnp.transpose(raw_part, (3, 1, 2, 0))) * (0.7 / math.sqrt(W * DP))
    out_index = lax.broadcasted_iota(jnp.int32, (DP, W, W, DP), 0)
    in_index = lax.broadcasted_iota(jnp.int32, (DP, W, W, DP), 3)
    right_chan = lax.broadcasted_iota(jnp.int32, (DP, W, W, DP), 1)
    left_chan = lax.broadcasted_iota(jnp.int32, (DP, W, W, DP), 2)
    identity_part = jnp.where((out_index == in_index) & (right_chan == 0) & (left_chan == 0), 1.0, 0.0).astype(jnp.float32)
    return (symmetric + identity_part).astype(jnp.bfloat16)


def steps_of(own_key, extent, shards, smallest, largest):
    level, own = 1.0, jax.random.fold_in(own_key, 6)
    for dim, parts in shards:
        heights = jnp.exp(jax.random.uniform(jax.random.fold_in(own, dim), (parts,), jnp.float32, smallest / len(shards), largest / len(shards)))
        level = level * jnp.repeat(heights, extent[dim] // parts).reshape([-1 if axis == dim else 1 for axis in range(len(extent))])
    return level


def scatter_about(own_key, extent, scale, limit, pieces=(), kind=jnp.bfloat16):
    factor_of = steps_of(own_key, extent, pieces, -0.22, 0.18) if pieces else 1.0
    result = jax.random.normal(own_key, extent, jnp.float32) * scale * factor_of
    return jnp.minimum(jnp.maximum(result, -limit), limit).astype(kind)


def setup_inputs(seed: int = 0) -> dict:
    key_list = jax.random.split(jax.random.key(seed), 5)
    left_env = draw_left_env(jax.random.fold_in(key_list[4], 71), 0)
    right_env = draw_right_env(jax.random.fold_in(key_list[4], 71), 0)
    site_operator = draw_site_operator(jax.random.fold_in(key_list[4], 71), 0)
    start_vector = scatter_about(key_list[3], (SEGS, D, DP, D), 1.0, 6.0, ((0, 8), (1, 4)), jnp.float32)
    return dict(left_env=left_env, right_env=right_env, site_operator=site_operator, start_vector=start_vector)


def apply_operator(left_one, operator_mat, right_mat, vector):
    lowered = vector.astype(jnp.bfloat16)
    contracted = jnp.dot(left_one.reshape(D * W, D), lowered.reshape(D, DP * D), preferred_element_type=jnp.float32)
    contracted = contracted.astype(jnp.bfloat16).reshape(D, W * DP, D)
    mixed = jnp.einsum('ik,akb->aib', operator_mat.astype(jnp.float32), contracted.astype(jnp.float32))
    mixed = mixed.astype(jnp.bfloat16).reshape(D, DP, W * D)
    return jnp.einsum('asc,bc->asb', mixed.astype(jnp.float32), right_mat.astype(jnp.float32))

def reference(left_env, right_env, site_operator, start_vector):
    operator_mat = site_operator.reshape(DP * W, W * DP)

    def one_segment(segment):
        left_one = left_env[segment]
        neighbour = jnp.minimum(segment + 1, SEGS - 1).astype(jnp.int32)
        right_mat = right_env[neighbour].reshape(D, W * D)
        start_one = start_vector[segment]
        current = start_one / jnp.sqrt(jnp.mean(start_one * start_one) + 1e-06)
        previous = jnp.zeros_like(current)
        beta_prev = jnp.zeros((), jnp.float32)
        alpha_list = []
        beta_list = []
        for step_index in range(ITERS):
            image = apply_operator(left_one, operator_mat, right_mat, current)
            alpha = jnp.mean(current * image)
            residual_vec = image - alpha * current - beta_prev * previous
            beta_next = jnp.sqrt(jnp.mean(residual_vec * residual_vec) + 1e-06)
            previous = current
            current = residual_vec / beta_next
            beta_prev = beta_next
            alpha_list.append(alpha)
            beta_list.append(beta_next)
        return (current, jnp.stack(alpha_list), jnp.stack(beta_list))
    vectors, alphas, betas_out = lax.map(one_segment, jnp.arange(SEGS, dtype=jnp.int32))
    return (vectors, alphas, betas_out)
```

```python
import functools

import jax
import jax.numpy as jnp
from jax import lax
from jax.experimental import pallas as pl
from jax.experimental.pallas import tpu as pltpu
from jax.sharding import PartitionSpec as P

ITERS = 2
GROUP = 16
CHUNKS = 4
MESH = pl.DeviceIdType.MESH


def kernel(
    n, segs, dp, width,
    l_ref, r_hbm, o_ref, x_ref,
    out_ref, scalar_ref,
    xg, t_ref, z_ref, r_ref, y_ref, q_ref, red,
    gsend, grecv, ssend, srecv, rsend, rrecv, rlocal,
):
    here, bond = l_ref.shape[1], l_ref.shape[2]
    entries = float(bond * dp * bond)
    seg, me = lax.axis_index("seg"), lax.axis_index("row")
    last = seg == segs - 1

    barrier = pltpu.get_barrier_semaphore()
    for k in range(1, n):
        pl.semaphore_signal(
            barrier, inc=1, device_id={"row": lax.rem(me + k, n)}, device_id_type=MESH
        )

    for k in (1, segs - 1):
        pl.semaphore_signal(
            barrier, inc=1, device_id={"seg": lax.rem(seg + k, segs)}, device_id_type=MESH
        )

    xg[0, :, pl.ds(me * here, here), :] = x_ref[...].astype(jnp.bfloat16).reshape(dp, here, bond)
    pl.semaphore_wait(barrier, n + 1)

    depth = width * bond // CHUNKS

    def right_copy(c):
        rows = pl.ds(c * depth, depth)
        return pltpu.make_async_remote_copy(
            src_ref=r_hbm.at[rows], dst_ref=r_ref.at[rows],
            send_sem=rsend.at[c], recv_sem=rrecv.at[c],
            device_id={"seg": seg - 1}, device_id_type=MESH,
        )

    def right_local(c):
        rows = pl.ds(c * depth, depth)
        return pltpu.make_async_copy(r_hbm.at[rows], r_ref.at[rows], rlocal.at[c])

    def vector_copy(it, way, step, block):
        rows = pl.ds(block * here, here)
        return pltpu.make_async_remote_copy(
            src_ref=xg.at[it, :, rows, :], dst_ref=xg.at[it, :, rows, :],
            send_sem=gsend.at[it, way, step], recv_sem=grecv.at[it, way, step],
            device_id={"row": me + (1 if way == 0 else -1)}, device_id_type=MESH,
        )

    def send_up(step):
        return jnp.logical_and(me < n - 1, me >= step)

    def send_down(step):
        return jnp.logical_and(me > 0, me + step <= n - 1)

    def gather_start(it, step):
        @pl.when(send_up(step))
        def _():
            vector_copy(it, 0, step, me - step).start()

        @pl.when(send_down(step))
        def _():
            vector_copy(it, 1, step, me + step).start()

    def gather_finish(it, step):
        @pl.when(me >= step + 1)
        def _():
            vector_copy(it, 0, step, me - 1 - step).wait_recv()

        @pl.when(me + 1 + step <= n - 1)
        def _():
            vector_copy(it, 1, step, me + 1 + step).wait_recv()

    def total(parts, it):
        row = lax.broadcasted_iota(jnp.int32, (8, 128), 0)
        tile = jnp.zeros((8, 128), jnp.float32)
        for i, part in enumerate(parts):
            tile = jnp.where(row == i, jnp.sum(part, keepdims=True), tile)
        red[it, me] = tile
        copies = []
        for k in range(1, n):
            copies.append(pltpu.make_async_remote_copy(
                src_ref=red.at[it, me], dst_ref=red.at[it, me],
                send_sem=ssend.at[it, k], recv_sem=srecv.at[it, k],
                device_id={"row": lax.rem(me + k, n)}, device_id_type=MESH,
            ))
        for copy in copies:
            copy.start()
        for k in range(1, n):
            other = lax.rem(me + n - k, n)
            pltpu.make_async_remote_copy(
                src_ref=red.at[it, other], dst_ref=red.at[it, other],
                send_sem=ssend.at[it, k], recv_sem=srecv.at[it, k],
                device_id={"row": other}, device_id_type=MESH,
            ).wait_recv()
        whole = red[it, 0]
        for j in range(1, n):
            whole = whole + red[it, j]
        for copy in copies:
            copy.wait_send()
        return [whole[i:i + 1, 0:1] for i in range(len(parts))]

    def apply(it):
        for step in range(n - 1):
            if step:
                gather_start(it, step)
            gather_finish(it, step)

        @pl.loop(0, dp * (width // 4))
        def _(i):
            r, m = i // (width // 4), i % (width // 4)
            rows = l_ref[pl.ds(m * 4, 4)].reshape(4 * here, bond)
            part = jnp.dot(rows, xg[it, r], preferred_element_type=jnp.float32)
            t_ref[r, pl.ds(m * 4, 4)] = part.astype(jnp.bfloat16).reshape(4, here, bond)

        @pl.loop(0, here // GROUP)
        def _(g):
            rows = pl.ds(pl.multiple_of(g * GROUP, GROUP), GROUP)
            t = t_ref[:, :, rows, :].reshape(dp * width * GROUP, bond)
            z = jnp.dot(o_ref[...], t, preferred_element_type=jnp.float32)
            z = z.astype(jnp.bfloat16).reshape(width, dp, GROUP, bond)
            for v in range(width):
                z_ref[:, rows, v * bond:(v + 1) * bond] = z[v]

        for c in range(CHUNKS):
            if it == 0:
                @pl.when(last)
                def _():
                    right_local(c).wait()

                @pl.when(jnp.logical_not(last))
                def _():
                    right_copy(c).wait_recv()

            z = z_ref[:, :, c * depth:(c + 1) * depth].reshape(dp * here, depth)
            part = jnp.dot(z, r_ref[c * depth:(c + 1) * depth, :], preferred_element_type=jnp.float32)
            if c == 0:
                y_ref[...] = part
            else:
                y_ref[...] += part

    gather_start(0, 0)
    for c in range(CHUNKS):
        @pl.when(seg > 0)
        def _():
            right_copy(c).start()

        @pl.when(last)
        def _():
            right_local(c).start()

    apply(0)
    x, y = x_ref[...], y_ref[...]
    xx, xy, yy = total([x * x, x * y, y * y], 0)
    inv = 1.0 / jnp.sqrt(xx / entries + 1e-06)
    xx, xy, yy = xx * inv * inv, xy * inv * inv, yy * inv * inv
    alpha0 = xy / entries
    beta0 = jnp.sqrt((yy - 2.0 * alpha0 * xy + alpha0 * alpha0 * xx) / entries + 1e-06)
    q = (y_ref[...] * inv - (alpha0 * inv) * x_ref[...]) * (1.0 / beta0)
    q_ref[...] = q
    xg[1, :, pl.ds(me * here, here), :] = q.astype(jnp.bfloat16).reshape(dp, here, bond)
    gather_start(1, 0)
    apply(1)
    x, y, q = x_ref[...] * inv, y_ref[...], q_ref[...]
    yy, yq, yx, qq, qx = total([y * y, y * q, y * x, q * q, q * x], 1)
    alpha1 = yq / entries
    norm = (
        yy - 2.0 * alpha1 * yq - 2.0 * beta0 * yx + alpha1 * alpha1 * qq
        + beta0 * beta0 * xx + 2.0 * alpha1 * beta0 * qx
    ) / entries
    beta1 = jnp.sqrt(norm + 1e-06)
    out_ref[...] = (
        y_ref[...] - alpha1 * q_ref[...] - (beta0 * inv) * x_ref[...]
    ) * (1.0 / beta1)
    row = lax.broadcasted_iota(jnp.int32, (8, 128), 0)
    tile = jnp.zeros((8, 128), jnp.float32)
    for i, value in enumerate((alpha0, alpha1, beta0, beta1)):
        tile = jnp.where(row == i, value, tile)
    scalar_ref[...] = tile

    for it in range(ITERS):
        for step in range(n - 1):
            @pl.when(send_up(step))
            def _():
                vector_copy(it, 0, step, me - step).wait_send()

            @pl.when(send_down(step))
            def _():
                vector_copy(it, 1, step, me + step).wait_send()
    for c in range(CHUNKS):
        @pl.when(seg > 0)
        def _():
            right_copy(c).wait_send()


def local(n, segs, left_env, right_env, site_operator, start_vector):
    _, here, width, bond = left_env.shape
    dp = site_operator.shape[0]
    left = jnp.transpose(left_env[0], (1, 0, 2))
    right = jnp.transpose(right_env[0], (1, 0, 2)).reshape(width * bond, bond)
    start = jnp.transpose(start_vector[0], (1, 0, 2)).reshape(dp * here, bond)
    mix = jnp.transpose(site_operator, (1, 0, 3, 2)).reshape(width * dp, dp * width)
    size = width * dp * GROUP
    wide = jnp.repeat(jnp.repeat(mix, GROUP, axis=0), GROUP, axis=1)
    row = lax.broadcasted_iota(jnp.int32, (size, size), 0) % GROUP
    col = lax.broadcasted_iota(jnp.int32, (size, size), 1) % GROUP
    wide = jnp.where(row == col, wide, jnp.zeros_like(wide))
    vmem = pl.BlockSpec(memory_space=pltpu.VMEM)
    dma = pltpu.SemaphoreType.DMA
    steps = max(n - 1, 1)
    result, scalars = pl.pallas_call(
        functools.partial(kernel, n, segs, dp, width),
        out_shape=(
            jax.ShapeDtypeStruct((dp * here, bond), jnp.float32),
            jax.ShapeDtypeStruct((8, 128), jnp.float32),
        ),
        in_specs=[vmem, pl.BlockSpec(memory_space=pl.ANY), vmem, vmem],
        out_specs=(vmem, vmem),
        scratch_shapes=[
            pltpu.VMEM((ITERS, dp, n * here, bond), jnp.bfloat16),
            pltpu.VMEM((dp, width, here, bond), jnp.bfloat16),
            pltpu.VMEM((dp, here, width * bond), jnp.bfloat16),
            pltpu.VMEM((width * bond, bond), jnp.bfloat16),
            pltpu.VMEM((dp * here, bond), jnp.float32),
            pltpu.VMEM((dp * here, bond), jnp.float32),
            pltpu.VMEM((ITERS, n, 8, 128), jnp.float32),
            dma((ITERS, 2, steps)), dma((ITERS, 2, steps)),
            dma((ITERS, n)), dma((ITERS, n)),
            dma((CHUNKS,)), dma((CHUNKS,)), dma((CHUNKS,)),
        ],
        compiler_params=pltpu.CompilerParams(
            collective_id=0, has_side_effects=True, vmem_limit_bytes=50 * 2**20
        ),
    )(left, right, wide, start)
    last = jnp.transpose(result.reshape(dp, here, bond), (1, 0, 2))[None]
    return last, scalars[0:2, 0].reshape(1, 2), scalars[2:4, 0].reshape(1, 2)


def solution(mesh):
    return jax.shard_map(
        functools.partial(local, mesh.shape["row"], mesh.shape["seg"]),
        mesh=mesh,
        in_specs=(
            P("seg", "row", None, None),
            P("seg", None, None, None),
            P(),
            P("seg", "row", None, None),
        ),
        out_specs=(P("seg", "row", None, None), P("seg", None), P("seg", None)),
        check_vma=False,
    )
```

```python
import functools

import jax
import jax.numpy as jnp
from jax import lax
from jax.experimental import pallas as pl
from jax.experimental.pallas import tpu as pltpu
from jax.sharding import PartitionSpec as P

ITERS = 2
GROUP = 16
CHUNKS = 4
MESH = pl.DeviceIdType.MESH


def kernel(
    n, segs, dp, width,
    l_ref, r_hbm, o_ref, x_ref,
    out_ref, scalar_ref,
    xg, t_ref, z_ref, r_ref, y_ref, q_ref, red,
    gsend, grecv, ssend, srecv, rsend, rrecv, rlocal,
):
    here, bond = l_ref.shape[1], l_ref.shape[2]
    entries = float(bond * dp * bond)
    seg, me = lax.axis_index("seg"), lax.axis_index("row")
    last = seg == segs - 1

    barrier = pltpu.get_barrier_semaphore()
    for k in range(1, n):
        pl.semaphore_signal(
            barrier, inc=1, device_id={"row": lax.rem(me + k, n)}, device_id_type=MESH
        )

    for k in (1, segs - 1):
        pl.semaphore_signal(
            barrier, inc=1, device_id={"seg": lax.rem(seg + k, segs)}, device_id_type=MESH
        )

    xg[0, :, pl.ds(me * here, here), :] = x_ref[...].astype(jnp.bfloat16).reshape(dp, here, bond)
    pl.semaphore_wait(barrier, n + 1)

    depth = width * bond // CHUNKS

    half = bond // 2
    each = width // CHUNKS

    def right_view(ref, c, part):
        if part == 0:
            return ref.at[pl.ds(c * each, each), pl.ds(0, half), :]
        return ref.at[pl.ds(c * each, each), pl.ds(half, half), pl.ds(half, half)]

    def right_copy(c, part):
        return pltpu.make_async_remote_copy(
            src_ref=right_view(r_hbm, c, part), dst_ref=right_view(r_ref, c, part),
            send_sem=rsend.at[c, part], recv_sem=rrecv.at[c, part],
            device_id={"seg": seg - 1}, device_id_type=MESH,
        )

    def right_local(c, part):
        return pltpu.make_async_copy(
            right_view(r_hbm, c, part), right_view(r_ref, c, part), rlocal.at[c, part]
        )

    def vector_copy(it, way, step, block):
        rows = pl.ds(block * here, here)
        return pltpu.make_async_remote_copy(
            src_ref=xg.at[it, :, rows, :], dst_ref=xg.at[it, :, rows, :],
            send_sem=gsend.at[it, way, step], recv_sem=grecv.at[it, way, step],
            device_id={"row": me + (1 if way == 0 else -1)}, device_id_type=MESH,
        )

    def send_up(step):
        return jnp.logical_and(me < n - 1, me >= step)

    def send_down(step):
        return jnp.logical_and(me > 0, me + step <= n - 1)

    def gather_start(it, step):
        @pl.when(send_up(step))
        def _():
            vector_copy(it, 0, step, me - step).start()

        @pl.when(send_down(step))
        def _():
            vector_copy(it, 1, step, me + step).start()

    def gather_finish(it, step):
        @pl.when(me >= step + 1)
        def _():
            vector_copy(it, 0, step, me - 1 - step).wait_recv()

        @pl.when(me + 1 + step <= n - 1)
        def _():
            vector_copy(it, 1, step, me + 1 + step).wait_recv()

    def total(parts, it):
        row = lax.broadcasted_iota(jnp.int32, (8, 128), 0)
        tile = jnp.zeros((8, 128), jnp.float32)
        for i, part in enumerate(parts):
            tile = jnp.where(row == i, jnp.sum(part, keepdims=True), tile)
        red[it, me] = tile
        copies = []
        for k in range(1, n):
            copies.append(pltpu.make_async_remote_copy(
                src_ref=red.at[it, me], dst_ref=red.at[it, me],
                send_sem=ssend.at[it, k], recv_sem=srecv.at[it, k],
                device_id={"row": lax.rem(me + k, n)}, device_id_type=MESH,
            ))
        for copy in copies:
            copy.start()
        for k in range(1, n):
            other = lax.rem(me + n - k, n)
            pltpu.make_async_remote_copy(
                src_ref=red.at[it, other], dst_ref=red.at[it, other],
                send_sem=ssend.at[it, k], recv_sem=srecv.at[it, k],
                device_id={"row": other}, device_id_type=MESH,
            ).wait_recv()
        whole = red[it, 0]
        for j in range(1, n):
            whole = whole + red[it, j]
        for copy in copies:
            copy.wait_send()
        return [whole[i:i + 1, 0:1] for i in range(len(parts))]

    def apply(it):
        for step in range(n - 1):
            if step:
                gather_start(it, step)
            gather_finish(it, step)

        @pl.loop(0, dp * (width // 4))
        def _(i):
            r, m = i // (width // 4), i % (width // 4)
            rows = l_ref[pl.ds(m * 4, 4)].reshape(4 * here, bond)
            part = jnp.dot(rows, xg[it, r], preferred_element_type=jnp.float32)
            t_ref[r, pl.ds(m * 4, 4)] = part.astype(jnp.bfloat16).reshape(4, here, bond)

        @pl.loop(0, here // GROUP)
        def _(g):
            rows = pl.ds(pl.multiple_of(g * GROUP, GROUP), GROUP)
            t = t_ref[:, :, rows, :].reshape(dp * width * GROUP, bond)
            z = jnp.dot(o_ref[...], t, preferred_element_type=jnp.float32)
            z = z.astype(jnp.bfloat16).reshape(width, dp, GROUP, bond)
            for v in range(width):
                z_ref[:, rows, v * bond:(v + 1) * bond] = z[v]

        for c in range(CHUNKS):
            if it == 0:
                @pl.when(last)
                def _():
                    for part in range(2):
                        right_local(c, part).wait()

                @pl.when(jnp.logical_not(last))
                def _():
                    for part in range(2):
                        right_copy(c, part).wait_recv()

                @pl.loop(c * each, (c + 1) * each)
                def _(v):
                    block = r_ref[v, 0:half, half:bond].astype(jnp.float32)
                    r_ref[v, half:bond, 0:half] = block.T.astype(jnp.bfloat16)

            z = z_ref[:, :, c * depth:(c + 1) * depth].reshape(dp * here, depth)
            part = jnp.dot(z, r_ref[c * each:(c + 1) * each].reshape(depth, bond), preferred_element_type=jnp.float32)
            if c == 0:
                y_ref[...] = part
            else:
                y_ref[...] += part

    gather_start(0, 0)
    for c in range(CHUNKS):
        @pl.when(seg > 0)
        def _():
            for part in range(2):
                right_copy(c, part).start()

        @pl.when(last)
        def _():
            for part in range(2):
                right_local(c, part).start()

    apply(0)
    x, y = x_ref[...], y_ref[...]
    xx, xy, yy = total([x * x, x * y, y * y], 0)
    inv = 1.0 / jnp.sqrt(xx / entries + 1e-06)
    xx, xy, yy = xx * inv * inv, xy * inv * inv, yy * inv * inv
    alpha0 = xy / entries
    beta0 = jnp.sqrt((yy - 2.0 * alpha0 * xy + alpha0 * alpha0 * xx) / entries + 1e-06)
    q = (y_ref[...] * inv - (alpha0 * inv) * x_ref[...]) * (1.0 / beta0)
    q_ref[...] = q
    xg[1, :, pl.ds(me * here, here), :] = q.astype(jnp.bfloat16).reshape(dp, here, bond)
    gather_start(1, 0)
    apply(1)
    x, y, q = x_ref[...] * inv, y_ref[...], q_ref[...]
    yy, yq, yx, qq, qx = total([y * y, y * q, y * x, q * q, q * x], 1)
    alpha1 = yq / entries
    norm = (
        yy - 2.0 * alpha1 * yq - 2.0 * beta0 * yx + alpha1 * alpha1 * qq
        + beta0 * beta0 * xx + 2.0 * alpha1 * beta0 * qx
    ) / entries
    beta1 = jnp.sqrt(norm + 1e-06)
    out_ref[...] = (
        y_ref[...] - alpha1 * q_ref[...] - (beta0 * inv) * x_ref[...]
    ) * (1.0 / beta1)
    row = lax.broadcasted_iota(jnp.int32, (8, 128), 0)
    tile = jnp.zeros((8, 128), jnp.float32)
    for i, value in enumerate((alpha0, alpha1, beta0, beta1)):
        tile = jnp.where(row == i, value, tile)
    scalar_ref[...] = tile

    for it in range(ITERS):
        for step in range(n - 1):
            @pl.when(send_up(step))
            def _():
                vector_copy(it, 0, step, me - step).wait_send()

            @pl.when(send_down(step))
            def _():
                vector_copy(it, 1, step, me + step).wait_send()
    for c in range(CHUNKS):
        @pl.when(seg > 0)
        def _():
            for part in range(2):
                right_copy(c, part).wait_send()


def local(n, segs, left_env, right_env, site_operator, start_vector):
    _, here, width, bond = left_env.shape
    dp = site_operator.shape[0]
    left = jnp.transpose(left_env[0], (1, 0, 2))
    right = jnp.transpose(right_env[0], (1, 0, 2))
    start = jnp.transpose(start_vector[0], (1, 0, 2)).reshape(dp * here, bond)
    mix = jnp.transpose(site_operator, (1, 0, 3, 2)).reshape(width * dp, dp * width)
    size = width * dp * GROUP
    wide = jnp.repeat(jnp.repeat(mix, GROUP, axis=0), GROUP, axis=1)
    row = lax.broadcasted_iota(jnp.int32, (size, size), 0) % GROUP
    col = lax.broadcasted_iota(jnp.int32, (size, size), 1) % GROUP
    wide = jnp.where(row == col, wide, jnp.zeros_like(wide))
    vmem = pl.BlockSpec(memory_space=pltpu.VMEM)
    dma = pltpu.SemaphoreType.DMA
    steps = max(n - 1, 1)
    result, scalars = pl.pallas_call(
        functools.partial(kernel, n, segs, dp, width),
        out_shape=(
            jax.ShapeDtypeStruct((dp * here, bond), jnp.float32),
            jax.ShapeDtypeStruct((8, 128), jnp.float32),
        ),
        in_specs=[vmem, pl.BlockSpec(memory_space=pl.ANY), vmem, vmem],
        out_specs=(vmem, vmem),
        scratch_shapes=[
            pltpu.VMEM((ITERS, dp, n * here, bond), jnp.bfloat16),
            pltpu.VMEM((dp, width, here, bond), jnp.bfloat16),
            pltpu.VMEM((dp, here, width * bond), jnp.bfloat16),
            pltpu.VMEM((width, bond, bond), jnp.bfloat16),
            pltpu.VMEM((dp * here, bond), jnp.float32),
            pltpu.VMEM((dp * here, bond), jnp.float32),
            pltpu.VMEM((ITERS, n, 8, 128), jnp.float32),
            dma((ITERS, 2, steps)), dma((ITERS, 2, steps)),
            dma((ITERS, n)), dma((ITERS, n)),
            dma((CHUNKS, 2)), dma((CHUNKS, 2)), dma((CHUNKS, 2)),
        ],
        compiler_params=pltpu.CompilerParams(
            collective_id=0, has_side_effects=True, vmem_limit_bytes=50 * 2**20
        ),
    )(left, right, wide, start)
    last = jnp.transpose(result.reshape(dp, here, bond), (1, 0, 2))[None]
    return last, scalars[0:2, 0].reshape(1, 2), scalars[2:4, 0].reshape(1, 2)


def solution(mesh):
    return jax.shard_map(
        functools.partial(local, mesh.shape["row"], mesh.shape["seg"]),
        mesh=mesh,
        in_specs=(
            P("seg", "row", None, None),
            P("seg", None, None, None),
            P(),
            P("seg", "row", None, None),
        ),
        out_specs=(P("seg", "row", None, None), P("seg", None), P("seg", None)),
        check_vma=False,
    )
```

```python
import functools

import jax
import jax.numpy as jnp
from jax import lax
from jax.experimental import pallas as pl
from jax.experimental.pallas import tpu as pltpu
from jax.sharding import PartitionSpec as P

ITERS = 2
GROUP = 16
CHUNKS = 4
MESH = pl.DeviceIdType.MESH


def kernel(
    n, segs, dp, width,
    l_ref, r_hbm, o_ref, x_ref,
    out_ref, scalar_ref,
    xg, t_ref, z_ref, r_ref, y_ref, q_ref, red,
    gsend, grecv, ssend, srecv, rsend, rrecv, rlocal,
):
    here, bond = l_ref.shape[1], l_ref.shape[2]
    entries = float(bond * dp * bond)
    seg, me = lax.axis_index("seg"), lax.axis_index("row")
    last = seg == segs - 1

    barrier = pltpu.get_barrier_semaphore()
    for k in range(1, n):
        pl.semaphore_signal(
            barrier, inc=1, device_id={"row": lax.rem(me + k, n)}, device_id_type=MESH
        )

    for k in (1, segs - 1):
        pl.semaphore_signal(
            barrier, inc=1, device_id={"seg": lax.rem(seg + k, segs)}, device_id_type=MESH
        )

    half = bond // 2

    def put(it, value):
        value = value.astype(jnp.bfloat16)
        for h in range(2):
            part = value[:, h * half:(h + 1) * half].reshape(dp, here, half)
            xg[it, h, :, pl.ds(me * here, here), :] = part

    put(0, x_ref[...])
    pl.semaphore_wait(barrier, n + 1)

    each = width // CHUNKS
    depth = each * half

    def right_view(ref, c, part):
        if part == 0:
            return ref.at[pl.ds(c * each, each), pl.ds(0, half), :]
        return ref.at[pl.ds(c * each, each), pl.ds(half, half), pl.ds(half, half)]

    def right_copy(c, part):
        return pltpu.make_async_remote_copy(
            src_ref=right_view(r_hbm, c, part), dst_ref=right_view(r_ref, c, part),
            send_sem=rsend.at[c, part], recv_sem=rrecv.at[c, part],
            device_id={"seg": seg - 1}, device_id_type=MESH,
        )

    def right_local(c, part):
        return pltpu.make_async_copy(
            right_view(r_hbm, c, part), right_view(r_ref, c, part), rlocal.at[c, part]
        )

    def vector_copy(it, h, way, step, block):
        rows = pl.ds(block * here, here)
        return pltpu.make_async_remote_copy(
            src_ref=xg.at[it, h, :, rows, :], dst_ref=xg.at[it, h, :, rows, :],
            send_sem=gsend.at[it, h, way, step], recv_sem=grecv.at[it, h, way, step],
            device_id={"row": me + (1 if way == 0 else -1)}, device_id_type=MESH,
        )

    def send_up(step):
        return jnp.logical_and(me < n - 1, me >= step)

    def send_down(step):
        return jnp.logical_and(me > 0, me + step <= n - 1)

    def gather_start(it, h, step):
        @pl.when(send_up(step))
        def _():
            vector_copy(it, h, 0, step, me - step).start()

        @pl.when(send_down(step))
        def _():
            vector_copy(it, h, 1, step, me + step).start()

    def gather_finish(it, h, step):
        @pl.when(me >= step + 1)
        def _():
            vector_copy(it, h, 0, step, me - 1 - step).wait_recv()

        @pl.when(me + 1 + step <= n - 1)
        def _():
            vector_copy(it, h, 1, step, me + 1 + step).wait_recv()

    def total(parts, it):
        row = lax.broadcasted_iota(jnp.int32, (8, 128), 0)
        tile = jnp.zeros((8, 128), jnp.float32)
        for i, part in enumerate(parts):
            tile = jnp.where(row == i, jnp.sum(part, keepdims=True), tile)
        red[it, me] = tile
        copies = []
        for k in range(1, n):
            copies.append(pltpu.make_async_remote_copy(
                src_ref=red.at[it, me], dst_ref=red.at[it, me],
                send_sem=ssend.at[it, k], recv_sem=srecv.at[it, k],
                device_id={"row": lax.rem(me + k, n)}, device_id_type=MESH,
            ))
        for copy in copies:
            copy.start()
        for k in range(1, n):
            other = lax.rem(me + n - k, n)
            pltpu.make_async_remote_copy(
                src_ref=red.at[it, other], dst_ref=red.at[it, other],
                send_sem=ssend.at[it, k], recv_sem=srecv.at[it, k],
                device_id={"row": other}, device_id_type=MESH,
            ).wait_recv()
        whole = red[it, 0]
        for j in range(1, n):
            whole = whole + red[it, j]
        for copy in copies:
            copy.wait_send()
        return [whole[i:i + 1, 0:1] for i in range(len(parts))]

    def lift(it, h):
        @pl.loop(0, dp * (width // 4))
        def _(i):
            r, m = i // (width // 4), i % (width // 4)
            rows = l_ref[pl.ds(m * 4, 4)].reshape(4 * here, bond)
            part = jnp.dot(rows, xg[it, h, r], preferred_element_type=jnp.float32)
            t_ref[r, pl.ds(m * 4, 4)] = part.astype(jnp.bfloat16).reshape(4, here, half)

        @pl.loop(0, here // GROUP)
        def _(g):
            rows = pl.ds(pl.multiple_of(g * GROUP, GROUP), GROUP)
            t = t_ref[:, :, rows, :].reshape(dp * width * GROUP, half)
            z = jnp.dot(o_ref[...], t, preferred_element_type=jnp.float32)
            z = z.astype(jnp.bfloat16).reshape(width, dp, GROUP, half)
            for v in range(width):
                z_ref[h, :, rows, v * half:(v + 1) * half] = z[v]

    def close(it, h):
        for c in range(CHUNKS):
            if it == 0:
                @pl.when(last)
                def _():
                    right_local(c, h).wait()

                @pl.when(jnp.logical_not(last))
                def _():
                    right_copy(c, h).wait_recv()

                if h == 1:
                    @pl.loop(c * each, (c + 1) * each)
                    def _(v):
                        block = r_ref[v, 0:half, half:bond].astype(jnp.float32)
                        r_ref[v, half:bond, 0:half] = block.T.astype(jnp.bfloat16)

            z = z_ref[h, :, :, c * depth:(c + 1) * depth].reshape(dp * here, depth)
            r = r_ref[c * each:(c + 1) * each, h * half:(h + 1) * half, :].reshape(depth, bond)
            part = jnp.dot(z, r, preferred_element_type=jnp.float32)
            if c == 0 and h == 0:
                y_ref[...] = part
            else:
                y_ref[...] += part

    def apply(it):
        for step in range(n - 1):
            if step:
                gather_start(it, 0, step)
            if step == n - 2:
                gather_start(it, 1, 0)
            gather_finish(it, 0, step)
        lift(it, 0)
        gather_finish(it, 1, 0)
        if n > 2:
            gather_start(it, 1, 1)
        if it > 0:
            close(it, 0)
        for step in range(1, n - 1):
            if step > 1:
                gather_start(it, 1, step)
            gather_finish(it, 1, step)
        lift(it, 1)
        if it == 0:
            close(it, 0)
        close(it, 1)

    gather_start(0, 0, 0)
    for part in range(2):
        for c in range(CHUNKS):
            @pl.when(seg > 0)
            def _():
                right_copy(c, part).start()

            @pl.when(last)
            def _():
                right_local(c, part).start()

    apply(0)
    x, y = x_ref[...], y_ref[...]
    xx, xy, yy = total([x * x, x * y, y * y], 0)
    inv = 1.0 / jnp.sqrt(xx / entries + 1e-06)
    xx, xy, yy = xx * inv * inv, xy * inv * inv, yy * inv * inv
    alpha0 = xy / entries
    beta0 = jnp.sqrt((yy - 2.0 * alpha0 * xy + alpha0 * alpha0 * xx) / entries + 1e-06)
    q = (y_ref[...] * inv - (alpha0 * inv) * x_ref[...]) * (1.0 / beta0)
    q_ref[...] = q
    put(1, q)
    gather_start(1, 0, 0)
    apply(1)
    x, y, q = x_ref[...] * inv, y_ref[...], q_ref[...]
    yy, yq, yx, qq, qx = total([y * y, y * q, y * x, q * q, q * x], 1)
    alpha1 = yq / entries
    norm = (
        yy - 2.0 * alpha1 * yq - 2.0 * beta0 * yx + alpha1 * alpha1 * qq
        + beta0 * beta0 * xx + 2.0 * alpha1 * beta0 * qx
    ) / entries
    beta1 = jnp.sqrt(norm + 1e-06)
    out_ref[...] = (
        y_ref[...] - alpha1 * q_ref[...] - (beta0 * inv) * x_ref[...]
    ) * (1.0 / beta1)
    row = lax.broadcasted_iota(jnp.int32, (8, 128), 0)
    tile = jnp.zeros((8, 128), jnp.float32)
    for i, value in enumerate((alpha0, alpha1, beta0, beta1)):
        tile = jnp.where(row == i, value, tile)
    scalar_ref[...] = tile

    for it, h in ((0, 0), (0, 1), (1, 0), (1, 1)):
        for step in range(n - 1):
            @pl.when(send_up(step))
            def _():
                vector_copy(it, h, 0, step, me - step).wait_send()

            @pl.when(send_down(step))
            def _():
                vector_copy(it, h, 1, step, me + step).wait_send()
    for c in range(CHUNKS):
        @pl.when(seg > 0)
        def _():
            for part in range(2):
                right_copy(c, part).wait_send()


def local(n, segs, left_env, right_env, site_operator, start_vector):
    _, here, width, bond = left_env.shape
    dp = site_operator.shape[0]
    left = jnp.transpose(left_env[0], (1, 0, 2))
    right = jnp.transpose(right_env[0], (1, 0, 2))
    start = jnp.transpose(start_vector[0], (1, 0, 2)).reshape(dp * here, bond)
    mix = jnp.transpose(site_operator, (1, 0, 3, 2)).reshape(width * dp, dp * width)
    size = width * dp * GROUP
    wide = jnp.repeat(jnp.repeat(mix, GROUP, axis=0), GROUP, axis=1)
    row = lax.broadcasted_iota(jnp.int32, (size, size), 0) % GROUP
    col = lax.broadcasted_iota(jnp.int32, (size, size), 1) % GROUP
    wide = jnp.where(row == col, wide, jnp.zeros_like(wide))
    vmem = pl.BlockSpec(memory_space=pltpu.VMEM)
    dma = pltpu.SemaphoreType.DMA
    steps = max(n - 1, 1)
    result, scalars = pl.pallas_call(
        functools.partial(kernel, n, segs, dp, width),
        out_shape=(
            jax.ShapeDtypeStruct((dp * here, bond), jnp.float32),
            jax.ShapeDtypeStruct((8, 128), jnp.float32),
        ),
        in_specs=[vmem, pl.BlockSpec(memory_space=pl.ANY), vmem, vmem],
        out_specs=(vmem, vmem),
        scratch_shapes=[
            pltpu.VMEM((ITERS, 2, dp, n * here, bond // 2), jnp.bfloat16),
            pltpu.VMEM((dp, width, here, bond // 2), jnp.bfloat16),
            pltpu.VMEM((2, dp, here, width * bond // 2), jnp.bfloat16),
            pltpu.VMEM((width, bond, bond), jnp.bfloat16),
            pltpu.VMEM((dp * here, bond), jnp.float32),
            pltpu.VMEM((dp * here, bond), jnp.float32),
            pltpu.VMEM((ITERS, n, 8, 128), jnp.float32),
            dma((ITERS, 2, 2, steps)), dma((ITERS, 2, 2, steps)),
            dma((ITERS, n)), dma((ITERS, n)),
            dma((CHUNKS, 2)), dma((CHUNKS, 2)), dma((CHUNKS, 2)),
        ],
        compiler_params=pltpu.CompilerParams(
            collective_id=0, has_side_effects=True, vmem_limit_bytes=50 * 2**20
        ),
    )(left, right, wide, start)
    last = jnp.transpose(result.reshape(dp, here, bond), (1, 0, 2))[None]
    return last, scalars[0:2, 0].reshape(1, 2), scalars[2:4, 0].reshape(1, 2)


def solution(mesh):
    return jax.shard_map(
        functools.partial(local, mesh.shape["row"], mesh.shape["seg"]),
        mesh=mesh,
        in_specs=(
            P("seg", "row", None, None),
            P("seg", None, None, None),
            P(),
            P("seg", "row", None, None),
        ),
        out_specs=(P("seg", "row", None, None), P("seg", None), P("seg", None)),
        check_vma=False,
    )
```

```python
import functools

import jax
import jax.numpy as jnp
from jax import lax
from jax.experimental import pallas as pl
from jax.experimental.pallas import tpu as pltpu
from jax.sharding import PartitionSpec as P

ITERS = 2
GROUP = 16
CHUNKS = 4
MESH = pl.DeviceIdType.MESH


def kernel(
    n, segs, dp, width,
    l_ref, r_hbm, o_ref, x_ref,
    out_ref, scalar_ref,
    xg, t_ref, z_ref, r_ref, y_ref, q_ref, red,
    gsend, grecv, ssend, srecv, rsend, rrecv, rlocal,
):
    here, bond = l_ref.shape[1], l_ref.shape[2]
    entries = float(bond * dp * bond)
    seg, me = lax.axis_index("seg"), lax.axis_index("row")
    last = seg == segs - 1

    barrier = pltpu.get_barrier_semaphore()
    for k in range(1, n):
        pl.semaphore_signal(
            barrier, inc=1, device_id={"row": lax.rem(me + k, n)}, device_id_type=MESH
        )

    for k in (1, segs - 1):
        pl.semaphore_signal(
            barrier, inc=1, device_id={"seg": lax.rem(seg + k, segs)}, device_id_type=MESH
        )

    half = bond // 2

    def put(it, value):
        value = value.astype(jnp.bfloat16)
        for h in range(2):
            part = value[:, h * half:(h + 1) * half].reshape(dp, here, half)
            xg[it, h, :, pl.ds(me * here, here), :] = part

    put(0, x_ref[...])
    pl.semaphore_wait(barrier, n + 1)

    each = width // CHUNKS
    depth = each * half

    def right_view(ref, c, part):
        if part == 0:
            return ref.at[pl.ds(c * each, each), pl.ds(0, half), :]
        return ref.at[pl.ds(c * each, each), pl.ds(half, half), pl.ds(half, half)]

    def right_copy(c, part):
        return pltpu.make_async_remote_copy(
            src_ref=right_view(r_hbm, c, part), dst_ref=right_view(r_ref, c, part),
            send_sem=rsend.at[c, part], recv_sem=rrecv.at[c, part],
            device_id={"seg": seg - 1}, device_id_type=MESH,
        )

    def right_local(c, part):
        return pltpu.make_async_copy(
            right_view(r_hbm, c, part), right_view(r_ref, c, part), rlocal.at[c, part]
        )

    def vector_copy(it, h, way, step, block):
        rows = pl.ds(block * here, here)
        return pltpu.make_async_remote_copy(
            src_ref=xg.at[it, h, :, rows, :], dst_ref=xg.at[it, h, :, rows, :],
            send_sem=gsend.at[it, h, way, step], recv_sem=grecv.at[it, h, way, step],
            device_id={"row": me + (1 if way == 0 else -1)}, device_id_type=MESH,
        )

    def send_up(step):
        return jnp.logical_and(me < n - 1, me >= step)

    def send_down(step):
        return jnp.logical_and(me > 0, me + step <= n - 1)

    def gather_start(it, h, step):
        @pl.when(send_up(step))
        def _():
            vector_copy(it, h, 0, step, me - step).start()

        @pl.when(send_down(step))
        def _():
            vector_copy(it, h, 1, step, me + step).start()

    def gather_finish(it, h, step):
        @pl.when(me >= step + 1)
        def _():
            vector_copy(it, h, 0, step, me - 1 - step).wait_recv()

        @pl.when(me + 1 + step <= n - 1)
        def _():
            vector_copy(it, h, 1, step, me + 1 + step).wait_recv()

    def total(parts, it):
        row = lax.broadcasted_iota(jnp.int32, (8, 128), 0)
        tile = jnp.zeros((8, 128), jnp.float32)
        for i, part in enumerate(parts):
            tile = jnp.where(row == i, jnp.sum(part, keepdims=True), tile)
        red[it, me] = tile
        copies = []
        for k in range(1, n):
            copies.append(pltpu.make_async_remote_copy(
                src_ref=red.at[it, me], dst_ref=red.at[it, me],
                send_sem=ssend.at[it, k], recv_sem=srecv.at[it, k],
                device_id={"row": lax.rem(me + k, n)}, device_id_type=MESH,
            ))
        for copy in copies:
            copy.start()
        for k in range(1, n):
            other = lax.rem(me + n - k, n)
            pltpu.make_async_remote_copy(
                src_ref=red.at[it, other], dst_ref=red.at[it, other],
                send_sem=ssend.at[it, k], recv_sem=srecv.at[it, k],
                device_id={"row": other}, device_id_type=MESH,
            ).wait_recv()
        whole = red[it, 0]
        for j in range(1, n):
            whole = whole + red[it, j]
        for copy in copies:
            copy.wait_send()
        return [whole[i:i + 1, 0:1] for i in range(len(parts))]

    def lift(it, h):
        @pl.loop(0, dp * (width // 4))
        def _(i):
            r, m = i // (width // 4), i % (width // 4)
            rows = l_ref[pl.ds(m * 4, 4)].reshape(4 * here, bond)
            part = jnp.dot(rows, xg[it, h, r], preferred_element_type=jnp.float32)
            t_ref[r, pl.ds(m * 4, 4)] = part.astype(jnp.bfloat16).reshape(4, here, half)

        @pl.loop(0, here // GROUP)
        def _(g):
            rows = pl.ds(pl.multiple_of(g * GROUP, GROUP), GROUP)
            t = t_ref[:, :, rows, :].reshape(dp * width * GROUP, half)
            z = jnp.dot(o_ref[...], t, preferred_element_type=jnp.float32)
            z = z.astype(jnp.bfloat16).reshape(width, dp, GROUP, half)
            for v in range(width):
                z_ref[h, :, rows, v * half:(v + 1) * half] = z[v]

    def close(it, h):
        for c in range(CHUNKS):
            if it == 0:
                @pl.when(last)
                def _():
                    right_local(c, h).wait()

                @pl.when(jnp.logical_not(last))
                def _():
                    right_copy(c, h).wait_recv()

                if h == 1:
                    @pl.loop(c * each, (c + 1) * each)
                    def _(v):
                        block = r_ref[v, 0:half, half:bond].astype(jnp.float32)
                        r_ref[v, half:bond, 0:half] = block.T.astype(jnp.bfloat16)

            z = z_ref[h, :, :, c * depth:(c + 1) * depth].reshape(dp * here, depth)
            r = r_ref[c * each:(c + 1) * each, h * half:(h + 1) * half, :].reshape(depth, bond)
            part = jnp.dot(z, r, preferred_element_type=jnp.float32)
            if c == 0 and h == 0:
                y_ref[...] = part
            else:
                y_ref[...] += part

    def apply(it):
        for step in range(n - 1):
            if step:
                gather_start(it, 0, step)
            if step == n - 2:
                gather_start(it, 1, 0)
            gather_finish(it, 0, step)
        gather_finish(it, 1, 0)
        if n > 2:
            gather_start(it, 1, 1)
        lift(it, 0)
        if n > 2:
            gather_finish(it, 1, 1)
        if n > 3:
            gather_start(it, 1, 2)
        if it > 0:
            close(it, 0)
        for step in range(2, n - 1):
            if step > 2:
                gather_start(it, 1, step)
            gather_finish(it, 1, step)
        lift(it, 1)
        if it == 0:
            close(it, 0)
        close(it, 1)

    gather_start(0, 0, 0)
    for part in range(2):
        for c in range(CHUNKS):
            @pl.when(seg > 0)
            def _():
                right_copy(c, part).start()

            @pl.when(last)
            def _():
                right_local(c, part).start()

    apply(0)
    x, y = x_ref[...], y_ref[...]
    xx, xy, yy = total([x * x, x * y, y * y], 0)
    inv = 1.0 / jnp.sqrt(xx / entries + 1e-06)
    xx, xy, yy = xx * inv * inv, xy * inv * inv, yy * inv * inv
    alpha0 = xy / entries
    beta0 = jnp.sqrt((yy - 2.0 * alpha0 * xy + alpha0 * alpha0 * xx) / entries + 1e-06)
    q = (y_ref[...] * inv - (alpha0 * inv) * x_ref[...]) * (1.0 / beta0)
    q_ref[...] = q
    put(1, q)
    gather_start(1, 0, 0)
    apply(1)
    x, y, q = x_ref[...] * inv, y_ref[...], q_ref[...]
    yy, yq, yx, qq, qx = total([y * y, y * q, y * x, q * q, q * x], 1)
    alpha1 = yq / entries
    norm = (
        yy - 2.0 * alpha1 * yq - 2.0 * beta0 * yx + alpha1 * alpha1 * qq
        + beta0 * beta0 * xx + 2.0 * alpha1 * beta0 * qx
    ) / entries
    beta1 = jnp.sqrt(norm + 1e-06)
    out_ref[...] = (
        y_ref[...] - alpha1 * q_ref[...] - (beta0 * inv) * x_ref[...]
    ) * (1.0 / beta1)
    row = lax.broadcasted_iota(jnp.int32, (8, 128), 0)
    tile = jnp.zeros((8, 128), jnp.float32)
    for i, value in enumerate((alpha0, alpha1, beta0, beta1)):
        tile = jnp.where(row == i, value, tile)
    scalar_ref[...] = tile

    for it, h in ((0, 0), (0, 1), (1, 0), (1, 1)):
        for step in range(n - 1):
            @pl.when(send_up(step))
            def _():
                vector_copy(it, h, 0, step, me - step).wait_send()

            @pl.when(send_down(step))
            def _():
                vector_copy(it, h, 1, step, me + step).wait_send()
    for c in range(CHUNKS):
        @pl.when(seg > 0)
        def _():
            for part in range(2):
                right_copy(c, part).wait_send()


def local(n, segs, left_env, right_env, site_operator, start_vector):
    _, here, width, bond = left_env.shape
    dp = site_operator.shape[0]
    left = jnp.transpose(left_env[0], (1, 0, 2))
    right = jnp.transpose(right_env[0], (1, 0, 2))
    start = jnp.transpose(start_vector[0], (1, 0, 2)).reshape(dp * here, bond)
    mix = jnp.transpose(site_operator, (1, 0, 3, 2)).reshape(width * dp, dp * width)
    size = width * dp * GROUP
    wide = jnp.repeat(jnp.repeat(mix, GROUP, axis=0), GROUP, axis=1)
    row = lax.broadcasted_iota(jnp.int32, (size, size), 0) % GROUP
    col = lax.broadcasted_iota(jnp.int32, (size, size), 1) % GROUP
    wide = jnp.where(row == col, wide, jnp.zeros_like(wide))
    vmem = pl.BlockSpec(memory_space=pltpu.VMEM)
    dma = pltpu.SemaphoreType.DMA
    steps = max(n - 1, 1)
    result, scalars = pl.pallas_call(
        functools.partial(kernel, n, segs, dp, width),
        out_shape=(
            jax.ShapeDtypeStruct((dp * here, bond), jnp.float32),
            jax.ShapeDtypeStruct((8, 128), jnp.float32),
        ),
        in_specs=[vmem, pl.BlockSpec(memory_space=pl.ANY), vmem, vmem],
        out_specs=(vmem, vmem),
        scratch_shapes=[
            pltpu.VMEM((ITERS, 2, dp, n * here, bond // 2), jnp.bfloat16),
            pltpu.VMEM((dp, width, here, bond // 2), jnp.bfloat16),
            pltpu.VMEM((2, dp, here, width * bond // 2), jnp.bfloat16),
            pltpu.VMEM((width, bond, bond), jnp.bfloat16),
            pltpu.VMEM((dp * here, bond), jnp.float32),
            pltpu.VMEM((dp * here, bond), jnp.float32),
            pltpu.VMEM((ITERS, n, 8, 128), jnp.float32),
            dma((ITERS, 2, 2, steps)), dma((ITERS, 2, 2, steps)),
            dma((ITERS, n)), dma((ITERS, n)),
            dma((CHUNKS, 2)), dma((CHUNKS, 2)), dma((CHUNKS, 2)),
        ],
        compiler_params=pltpu.CompilerParams(
            collective_id=0, has_side_effects=True, vmem_limit_bytes=50 * 2**20
        ),
    )(left, right, wide, start)
    last = jnp.transpose(result.reshape(dp, here, bond), (1, 0, 2))[None]
    return last, scalars[0:2, 0].reshape(1, 2), scalars[2:4, 0].reshape(1, 2)


def solution(mesh):
    return jax.shard_map(
        functools.partial(local, mesh.shape["row"], mesh.shape["seg"]),
        mesh=mesh,
        in_specs=(
            P("seg", "row", None, None),
            P("seg", None, None, None),
            P(),
            P("seg", "row", None, None),
        ),
        out_specs=(P("seg", "row", None, None), P("seg", None), P("seg", None)),
        check_vma=False,
    )
```

```python
import functools

import jax
import jax.numpy as jnp
from jax import lax
from jax.experimental import pallas as pl
from jax.experimental.pallas import tpu as pltpu
from jax.sharding import PartitionSpec as P

ITERS = 2
GROUP = 16
CHUNKS = 4
MESH = pl.DeviceIdType.MESH


def kernel(
    n, segs, dp, width,
    l_ref, r_hbm, o_ref, x_ref,
    out_ref, scalar_ref,
    xg, t_ref, z_ref, r_ref, y_ref, q_ref, red,
    gsend, grecv, ssend, srecv, rsend, rrecv, rlocal,
):
    here, bond = l_ref.shape[1], l_ref.shape[2]
    entries = float(bond * dp * bond)
    seg, me = lax.axis_index("seg"), lax.axis_index("row")
    last = seg == segs - 1

    barrier = pltpu.get_barrier_semaphore()
    for k in range(1, n):
        pl.semaphore_signal(
            barrier, inc=1, device_id={"row": lax.rem(me + k, n)}, device_id_type=MESH
        )

    for k in (1, segs - 1):
        pl.semaphore_signal(
            barrier, inc=1, device_id={"seg": lax.rem(seg + k, segs)}, device_id_type=MESH
        )

    half, quarter = bond // 2, bond // 4

    def put(it, value):
        value = value.astype(jnp.bfloat16)
        for h in range(2):
            part = value[:, h * half:(h + 1) * half].reshape(dp, here, half)
            xg[it, h, :, pl.ds(me * here, here), :] = part

    put(0, x_ref[...])
    pl.semaphore_wait(barrier, n + 1)

    each = width // CHUNKS
    depth = each * half

    def right_view(ref, c, part):
        rows, columns = pl.ds(part * quarter, quarter), pl.ds(part * quarter, bond - part * quarter)
        return ref.at[pl.ds(c * each, each), rows, columns]

    def right_copy(c, part):
        return pltpu.make_async_remote_copy(
            src_ref=right_view(r_hbm, c, part), dst_ref=right_view(r_ref, c, part),
            send_sem=rsend.at[c, part], recv_sem=rrecv.at[c, part],
            device_id={"seg": seg - 1}, device_id_type=MESH,
        )

    def right_local(c, part):
        return pltpu.make_async_copy(
            right_view(r_hbm, c, part), right_view(r_ref, c, part), rlocal.at[c, part]
        )

    def vector_copy(it, h, way, step, block):
        rows = pl.ds(block * here, here)
        return pltpu.make_async_remote_copy(
            src_ref=xg.at[it, h, :, rows, :], dst_ref=xg.at[it, h, :, rows, :],
            send_sem=gsend.at[it, h, way, step], recv_sem=grecv.at[it, h, way, step],
            device_id={"row": me + (1 if way == 0 else -1)}, device_id_type=MESH,
        )

    def send_up(step):
        return jnp.logical_and(me < n - 1, me >= step)

    def send_down(step):
        return jnp.logical_and(me > 0, me + step <= n - 1)

    def gather_start(it, h, step):
        @pl.when(send_up(step))
        def _():
            vector_copy(it, h, 0, step, me - step).start()

        @pl.when(send_down(step))
        def _():
            vector_copy(it, h, 1, step, me + step).start()

    def gather_finish(it, h, step):
        @pl.when(me >= step + 1)
        def _():
            vector_copy(it, h, 0, step, me - 1 - step).wait_recv()

        @pl.when(me + 1 + step <= n - 1)
        def _():
            vector_copy(it, h, 1, step, me + 1 + step).wait_recv()

    def total(parts, it):
        row = lax.broadcasted_iota(jnp.int32, (8, 128), 0)
        tile = jnp.zeros((8, 128), jnp.float32)
        for i, part in enumerate(parts):
            tile = jnp.where(row == i, jnp.sum(part, keepdims=True), tile)
        red[it, me] = tile
        copies = []
        for k in range(1, n):
            copies.append(pltpu.make_async_remote_copy(
                src_ref=red.at[it, me], dst_ref=red.at[it, me],
                send_sem=ssend.at[it, k], recv_sem=srecv.at[it, k],
                device_id={"row": lax.rem(me + k, n)}, device_id_type=MESH,
            ))
        for copy in copies:
            copy.start()
        for k in range(1, n):
            other = lax.rem(me + n - k, n)
            pltpu.make_async_remote_copy(
                src_ref=red.at[it, other], dst_ref=red.at[it, other],
                send_sem=ssend.at[it, k], recv_sem=srecv.at[it, k],
                device_id={"row": other}, device_id_type=MESH,
            ).wait_recv()
        whole = red[it, 0]
        for j in range(1, n):
            whole = whole + red[it, j]
        for copy in copies:
            copy.wait_send()
        return [whole[i:i + 1, 0:1] for i in range(len(parts))]

    def lift(it, h):
        @pl.loop(0, dp * (width // 4))
        def _(i):
            r, m = i // (width // 4), i % (width // 4)
            rows = l_ref[pl.ds(m * 4, 4)].reshape(4 * here, bond)
            part = jnp.dot(rows, xg[it, h, r], preferred_element_type=jnp.float32)
            t_ref[r, pl.ds(m * 4, 4)] = part.astype(jnp.bfloat16).reshape(4, here, half)

        @pl.loop(0, here // GROUP)
        def _(g):
            rows = pl.ds(pl.multiple_of(g * GROUP, GROUP), GROUP)
            t = t_ref[:, :, rows, :].reshape(dp * width * GROUP, half)
            z = jnp.dot(o_ref[...], t, preferred_element_type=jnp.float32)
            z = z.astype(jnp.bfloat16).reshape(width, dp, GROUP, half)
            for v in range(width):
                z_ref[h, :, rows, v * half:(v + 1) * half] = z[v]

    def close(it, h):
        for c in range(CHUNKS):
            if it == 0:
                parts = (2 * h, 2 * h + 1)

                @pl.when(last)
                def _():
                    for part in parts:
                        right_local(c, part).wait()

                @pl.when(jnp.logical_not(last))
                def _():
                    for part in parts:
                        right_copy(c, part).wait_recv()

                @pl.loop(c * each, (c + 1) * each)
                def _(v):
                    for part in parts:
                        if part > 0:
                            edge = part * quarter
                            block = r_ref[v, 0:edge, edge:edge + quarter].astype(jnp.float32)
                            r_ref[v, edge:edge + quarter, 0:edge] = block.T.astype(jnp.bfloat16)

            z = z_ref[h, :, :, c * depth:(c + 1) * depth].reshape(dp * here, depth)
            r = r_ref[c * each:(c + 1) * each, h * half:(h + 1) * half, :].reshape(depth, bond)
            part = jnp.dot(z, r, preferred_element_type=jnp.float32)
            if c == 0 and h == 0:
                y_ref[...] = part
            else:
                y_ref[...] += part

    def apply(it):
        for step in range(n - 1):
            if step:
                gather_start(it, 0, step)
            if step == n - 2:
                gather_start(it, 1, 0)
            gather_finish(it, 0, step)
        gather_finish(it, 1, 0)
        if n > 2:
            gather_start(it, 1, 1)
        lift(it, 0)
        if n > 2:
            gather_finish(it, 1, 1)
        if n > 3:
            gather_start(it, 1, 2)
        if it > 0:
            close(it, 0)
        for step in range(2, n - 1):
            if step > 2:
                gather_start(it, 1, step)
            gather_finish(it, 1, step)
        lift(it, 1)
        if it == 0:
            close(it, 0)
        close(it, 1)

    gather_start(0, 0, 0)
    for h in range(2):
        for c in range(CHUNKS):
            @pl.when(seg > 0)
            def _():
                for part in (2 * h, 2 * h + 1):
                    right_copy(c, part).start()

            @pl.when(last)
            def _():
                for part in (2 * h, 2 * h + 1):
                    right_local(c, part).start()

    apply(0)
    x, y = x_ref[...], y_ref[...]
    xx, xy, yy = total([x * x, x * y, y * y], 0)
    inv = 1.0 / jnp.sqrt(xx / entries + 1e-06)
    xx, xy, yy = xx * inv * inv, xy * inv * inv, yy * inv * inv
    alpha0 = xy / entries
    beta0 = jnp.sqrt((yy - 2.0 * alpha0 * xy + alpha0 * alpha0 * xx) / entries + 1e-06)
    q = (y_ref[...] * inv - (alpha0 * inv) * x_ref[...]) * (1.0 / beta0)
    q_ref[...] = q
    put(1, q)
    gather_start(1, 0, 0)
    apply(1)
    x, y, q = x_ref[...] * inv, y_ref[...], q_ref[...]
    yy, yq, yx, qq, qx = total([y * y, y * q, y * x, q * q, q * x], 1)
    alpha1 = yq / entries
    norm = (
        yy - 2.0 * alpha1 * yq - 2.0 * beta0 * yx + alpha1 * alpha1 * qq
        + beta0 * beta0 * xx + 2.0 * alpha1 * beta0 * qx
    ) / entries
    beta1 = jnp.sqrt(norm + 1e-06)
    out_ref[...] = (
        y_ref[...] - alpha1 * q_ref[...] - (beta0 * inv) * x_ref[...]
    ) * (1.0 / beta1)
    row = lax.broadcasted_iota(jnp.int32, (8, 128), 0)
    tile = jnp.zeros((8, 128), jnp.float32)
    for i, value in enumerate((alpha0, alpha1, beta0, beta1)):
        tile = jnp.where(row == i, value, tile)
    scalar_ref[...] = tile

    for it, h in ((0, 0), (0, 1), (1, 0), (1, 1)):
        for step in range(n - 1):
            @pl.when(send_up(step))
            def _():
                vector_copy(it, h, 0, step, me - step).wait_send()

            @pl.when(send_down(step))
            def _():
                vector_copy(it, h, 1, step, me + step).wait_send()
    for c in range(CHUNKS):
        @pl.when(seg > 0)
        def _():
            for part in range(4):
                right_copy(c, part).wait_send()


def local(n, segs, left_env, right_env, site_operator, start_vector):
    _, here, width, bond = left_env.shape
    dp = site_operator.shape[0]
    left = jnp.transpose(left_env[0], (1, 0, 2))
    right = jnp.transpose(right_env[0], (1, 0, 2))
    start = jnp.transpose(start_vector[0], (1, 0, 2)).reshape(dp * here, bond)
    mix = jnp.transpose(site_operator, (1, 0, 3, 2)).reshape(width * dp, dp * width)
    size = width * dp * GROUP
    wide = jnp.repeat(jnp.repeat(mix, GROUP, axis=0), GROUP, axis=1)
    row = lax.broadcasted_iota(jnp.int32, (size, size), 0) % GROUP
    col = lax.broadcasted_iota(jnp.int32, (size, size), 1) % GROUP
    wide = jnp.where(row == col, wide, jnp.zeros_like(wide))
    vmem = pl.BlockSpec(memory_space=pltpu.VMEM)
    dma = pltpu.SemaphoreType.DMA
    steps = max(n - 1, 1)
    result, scalars = pl.pallas_call(
        functools.partial(kernel, n, segs, dp, width),
        out_shape=(
            jax.ShapeDtypeStruct((dp * here, bond), jnp.float32),
            jax.ShapeDtypeStruct((8, 128), jnp.float32),
        ),
        in_specs=[vmem, pl.BlockSpec(memory_space=pl.ANY), vmem, vmem],
        out_specs=(vmem, vmem),
        scratch_shapes=[
            pltpu.VMEM((ITERS, 2, dp, n * here, bond // 2), jnp.bfloat16),
            pltpu.VMEM((dp, width, here, bond // 2), jnp.bfloat16),
            pltpu.VMEM((2, dp, here, width * bond // 2), jnp.bfloat16),
            pltpu.VMEM((width, bond, bond), jnp.bfloat16),
            pltpu.VMEM((dp * here, bond), jnp.float32),
            pltpu.VMEM((dp * here, bond), jnp.float32),
            pltpu.VMEM((ITERS, n, 8, 128), jnp.float32),
            dma((ITERS, 2, 2, steps)), dma((ITERS, 2, 2, steps)),
            dma((ITERS, n)), dma((ITERS, n)),
            dma((CHUNKS, 4)), dma((CHUNKS, 4)), dma((CHUNKS, 4)),
        ],
        compiler_params=pltpu.CompilerParams(
            collective_id=0, has_side_effects=True, vmem_limit_bytes=50 * 2**20
        ),
    )(left, right, wide, start)
    last = jnp.transpose(result.reshape(dp, here, bond), (1, 0, 2))[None]
    return last, scalars[0:2, 0].reshape(1, 2), scalars[2:4, 0].reshape(1, 2)


def solution(mesh):
    return jax.shard_map(
        functools.partial(local, mesh.shape["row"], mesh.shape["seg"]),
        mesh=mesh,
        in_specs=(
            P("seg", "row", None, None),
            P("seg", None, None, None),
            P(),
            P("seg", "row", None, None),
        ),
        out_specs=(P("seg", "row", None, None), P("seg", None), P("seg", None)),
        check_vma=False,
    )
```
